32 devices in a mesh: groups: 2 (over y), node: 4 (over x, core), local: 4 (over z).
Axes of the slice: x: 2, y: 2, z: 4, core: 2. Of those that a mesh axis runs over, the one named last changes fastest.
Arguments:
- residual: bfloat16 [4, 512, 2048], P(None, ('groups', 'node', 'local')), parts along dimension 1, may hold values from -24 to 24
- query: bfloat16 [4, 512, 2048], P(None, ('groups', 'node', 'local')), parts along dimension 1, may hold values from -15 to 15
- new_keys: bfloat16 [4, 512, 256], P(None, ('groups', 'node', 'local')), parts along dimension 1, may hold values from -6 to 6
- new_values: bfloat16 [4, 512, 256], P(None, ('groups', 'node', 'local')), parts along dimension 1, may hold values from -6 to 6
- key_cache: bfloat16 [512, 80, 256], P(('groups', 'node', 'local')), parts along dimension 0, may hold values from -15 to 15
- value_cache: bfloat16 [512, 80, 256], P(('groups', 'node', 'local')), parts along dimension 0, may hold values from -6 to 6
- lengths: int32 [512], P(('groups', 'node', 'local')), parts along dimension 0, may hold values from 2 to 76
- norm_gain: float32 [2048], replicated, may hold values from 0.5 to 1.5
- expert_ids: int32 [4, 512, 8], P(None, ('groups', 'node', 'local')), parts along dimension 1, may hold values from 0 to 15, all different within a row; in each aligned block of 16 rows (0 to 15, 16 to 31, ..., all dimensions but the last counted through in order) at most 16 rows name the same one
- gate_scores: float32 [4, 512, 8], P(None, ('groups', 'node', 'local')), parts along dimension 1, may hold values from 0.05 to 1
- learner_gate: float32 [16, 2048, 384], P(None, ('node', 'local')), may hold values from -0.125 to 0.125
- learner_up: float32 [16, 2048, 384], P(None, ('node', 'local')), may hold values from -0.125 to 0.125
- learner_down: float32 [16, 2048, 384], P(None, ('node', 'local')), may hold values from -0.625 to 0.625
Outputs:
- mixture: bfloat16 [4, 512, 2048], P(None, ('groups', 'node', 'local')), parts along dimension 1
- stream: bfloat16 [4, 512, 2048], P(None, ('groups', 'node', 'local')), parts along dimension 1
The draws below stay inside these ranges and needn't reach their ends.
There are 2 independent parts, one for each index of `groups`. The reference program is written for one: setup_inputs(seed, part) draws one part's arguments, and reference() takes and returns one part's arrays. A program takes and returns all parts, laid end to end along the dimension named above; an argument that names none is the same for every part. Nothing has to cross between parts.
Inputs may be any that keep to these rules, and one draw needn't show every extreme that they name: `expert_ids`: each row names 8 different experts; in one step, no expert is named by more than 16 of the 16 rows that one device holds.
All inputs are finite; a program needn't handle non-finite values.
Results may differ from the reference program's by a relative error of at most 0.0087.
Values may be sent and summed in bfloat16 or wider, within the bound.
A program may use at most 128 MiB of HBM per device.

```python
import math
from functools import partial
import jax
import jax.numpy as jnp
import numpy as np
from jax import lax

D = 2048
HEADS = 16
KV_HEADS = 2
HEAD_DIM = 128
FFE = 384
TOPK = 8
STEPS = 4
R_DEV = 16
CACHE = 80
EXPERTS = 16
ROWS = 256
CAP = 16
N_NODE = 4
N_LOCAL = 4


def draw_query(key, part):
    own_key = jax.random.fold_in(key, 13)
    row_width = HEADS * HEAD_DIM
    return jnp.clip(jax.random.normal(own_key, (STEPS, ROWS, row_width), jnp.float32), -6.0, 6.0).astype(jnp.bfloat16)


def draw_key_cache(key, part):
    own_key = jax.random.fold_in(key, 11)
    row_width = KV_HEADS * HEAD_DIM
    return jnp.clip(jax.random.normal(own_key, (ROWS, CACHE, row_width), jnp.float32), -6.0, 6.0).astype(jnp.bfloat16)


def draw_residual(key, part):
    own_key = jax.random.fold_in(key, 17)
    column_scale = jnp.exp(jax.random.uniform(jax.random.fold_in(own_key, 1), (D,), jnp.float32, math.log(0.3), math.log(3.0)))
    row_scale = jnp.exp(jax.random.uniform(jax.random.fold_in(own_key, 2), (STEPS, ROWS, 1), jnp.float32, math.log(0.5), math.log(2.0)))
    values = jnp.clip(jax.random.normal(jax.random.fold_in(own_key, 3), (STEPS, ROWS, D), jnp.float32), -4.0, 4.0)
    return (values * column_scale * row_scale).astype(jnp.bfloat16)


def with_ends(drawn, stream_key, least, largest):
    spot = [jax.random.randint(jax.random.fold_in(stream_key, axis), (), 0, length) for axis, length in enumerate(drawn.shape)]
    longest = drawn.shape.index(max(drawn.shape))
    beside = spot[:longest] + [(spot[longest] + 1) % drawn.shape[longest]] + spot[longest + 1:]
    return drawn.at[tuple(spot)].set(least).at[tuple(beside)].set(largest)


def levels(key, dims, split, least, top_value):
    def one(position, shards_of):
        heights = jax.random.uniform(jax.random.fold_in(jax.random.fold_in(key, 6), position), (shards_of,), jnp.float32, least / len(split), top_value / len(split))
        return jnp.repeat(jnp.exp(heights), dims[position] // shards_of).reshape((-1,) + (1,) * (len(dims) - position - 1))

    loudness = one(*split[0])
    for cut in split[1:]:
        loudness = loudness * one(*cut)
    return loudness


def assign_block(stream_key, own, number, rows, number_of, top, reach, slope):
    sequence = jax.random.permutation(stream_key, number_of)
    heavy_load, usual = load_shares(number_of, rows * top, reach, slope, True), load_shares(number_of, rows * top, reach, slope, False)
    places = jnp.arange(number_of)

    def named(tallies, rotation):
        used = int((tallies > 0).sum())
        fixed = max(1, used // 4)
        shifted = fixed + (places - fixed + rotation * (used - fixed)) % max(1, number_of - fixed)
        return jnp.zeros((number_of,), jnp.int32).at[sequence[jnp.where(places < fixed, places, shifted)]].set(jnp.asarray(tallies, jnp.int32))

    tallies = jnp.where(number % 4 == 0, named(heavy_load, number // 4), named(usual, number - number // 4 - 1))
    mixed = jax.random.permutation(jax.random.fold_in(own, 3), number_of)
    source_of, receiver = mixed[0:number_of // 2 * 2:2], mixed[1:number_of // 2 * 2:2]
    margin = jnp.minimum(tallies[source_of] - 1, reach - tallies[receiver]) // 2
    margin = jnp.where((source_of == sequence[0]) | (receiver == sequence[0]) | (tallies[receiver] == 0), 0, jnp.maximum(margin, 0))
    shifted = jax.random.randint(jax.random.fold_in(own, 4), (number_of // 2,), 0, 1 << 20) % (margin + 1)
    tallies = tallies.at[source_of].add(-shifted).at[receiver].add(shifted)
    labels = jnp.searchsorted(jnp.cumsum(tallies), jnp.arange(rows * top), side="right").astype(jnp.int32)
    table = labels.reshape(top, rows).T
    table = table[jax.random.permutation(jax.random.fold_in(own, 1), rows)]
    rotation = jax.random.randint(jax.random.fold_in(own, 2), (rows, 1), 0, top)
    return jnp.take_along_axis(table, (jnp.arange(top)[None, :] + rotation) % top, axis=1)


def load_shares(amount, total, bound, slope, full):
    weights = [(1 << 20) // math.isqrt(grade ** slope) + 1 for grade in range(1, amount + 1)]
    largest = bound if full else min(bound, max(-(-total // amount), total * weights[0] // sum(weights)))
    least = 1 if total - largest >= amount - 1 else 0
    given, rest = [largest] + [least] * (amount - 1), total - largest - least * (amount - 1)
    while rest > 0:
        free = [i for i in range(1, amount) if given[i] < largest] or [i for i in range(1, amount) if given[i] < bound]
        pool, remaining = sum([weights[i] for i in free]), rest
        for i in free:
            addition = min(bound - given[i], max(1, remaining * weights[i] // pool), rest)
            given[i] = given[i] + addition
            rest = rest - addition
    return np.array(given)


def gaussian(key, extent, scale, reach, shards=(), kind=jnp.bfloat16):
    array = scale * jax.random.normal(key, extent, jnp.float32)
    if shards:
        array = array * levels(key, extent, shards, -0.22, 0.18)
    return jnp.clip(array, -reach, reach).astype(kind)


def setup_inputs(seed: int = 0, part: int = 0) -> dict:
    keys = jax.random.split(jax.random.key(seed), 14)
    part_keys = jax.random.split(jax.random.fold_in(keys[13], part), 14)
    residual = draw_residual(jax.random.fold_in(jax.random.fold_in(keys[13], part), 71), part)
    query = draw_query(jax.random.fold_in(jax.random.fold_in(keys[13], part), 71), part)
    new_keys = gaussian(part_keys[2], (STEPS, ROWS, KV_HEADS * HEAD_DIM), 1.0, 6.0, ((1, 16),))
    new_values = gaussian(part_keys[3], (STEPS, ROWS, KV_HEADS * HEAD_DIM), 1.0, 6.0, ((1, 16),))
    key_cache = draw_key_cache(jax.random.fold_in(jax.random.fold_in(keys[13], part), 71), part)
    value_cache = gaussian(part_keys[5], (ROWS, CACHE, KV_HEADS * HEAD_DIM), 1.0, 6.0, ((0, 16),))
    lengths = with_ends(jax.random.randint(part_keys[6], (ROWS,), 2, CACHE - STEPS + 1), jax.random.fold_in(part_keys[6], 1), 2, CACHE - STEPS).astype(jnp.int32)
    norm_gain = jnp.clip(1.0 + 0.1 * jax.random.normal(keys[7], (D,), jnp.float32), 0.5, 1.5)
    expert_ids_keys = jax.random.split(jax.random.fold_in(part_keys[8], 1), STEPS * ROWS // R_DEV)
    expert_ids_turns = jax.random.permutation(jax.random.fold_in(part_keys[8], 3), STEPS * ROWS // R_DEV)
    expert_ids = jax.vmap(lambda own, number: assign_block(jax.random.fold_in(part_keys[8], 2), own, number, R_DEV, EXPERTS, TOPK, CAP, 2))(expert_ids_keys, expert_ids_turns).reshape((STEPS, ROWS, TOPK))
    gate_scores = jnp.clip(jnp.exp(math.log(1.0) - 2.9957323 * jax.random.uniform(part_keys[9], (STEPS, ROWS, TOPK), jnp.float32) ** levels(part_keys[9], (STEPS, ROWS, TOPK), ((1, 16),), -0.2, 0.2)), 0.05, 1.0)
    learner_gate = gaussian(keys[10], (EXPERTS, D, FFE), D ** -0.5, 0.125, ((1, 16),), jnp.float32)
    learner_up = gaussian(keys[11], (EXPERTS, D, FFE), D ** -0.5, 0.125, ((1, 16),), jnp.float32)
    learner_down = gaussian(keys[12], (EXPERTS, D, FFE), (FFE // 4) ** -0.5, 0.625, ((1, 16),), jnp.float32)
    return {"residual": residual, "query": query, "new_keys": new_keys, "new_values": new_values, "key_cache": key_cache, "value_cache": value_cache, "lengths": lengths, "norm_gain": norm_gain, "expert_ids": expert_ids, "gate_scores": gate_scores, "learner_gate": learner_gate, "learner_up": learner_up, "learner_down": learner_down}


epsilon = 1e-06

def place_rows(expert_list, expert_count, capacity):
    targets = jnp.arange(expert_count, dtype=jnp.int32)
    matches = (expert_list[:, :, None] == targets).astype(jnp.int32)
    counts = lax.optimization_barrier(jnp.sum(matches, axis=1, dtype=jnp.int32))
    earlier = jnp.cumsum(counts, axis=0, dtype=jnp.int32) - counts
    ranked = lax.optimization_barrier(jnp.sum(matches * earlier[:, None, :], axis=2, dtype=jnp.int32))
    return jnp.where(expert_list >= 0, expert_list * capacity + ranked, -1).astype(jnp.int32)

def attend(query_now, cache_keys, cache_values, fresh_keys, fresh_values, lengths, step_index):
    row_count = query_now.shape[0]
    group_size = HEADS // KV_HEADS
    queries = query_now.astype(jnp.float32).reshape(row_count, KV_HEADS, group_size, HEAD_DIM)
    score_scale = 1.0 / math.sqrt(HEAD_DIM)
    cache_scores = jnp.einsum('rgqd,rcgd->rgqc', queries, cache_keys) * score_scale
    fresh_scores = jnp.einsum('rgqd,rjgd->rgqj', queries, fresh_keys) * score_scale
    positions = jnp.arange(cache_keys.shape[1], dtype=jnp.int32)
    cache_live = positions[None, :] < lengths[:, None]
    fresh_live = jnp.arange(fresh_keys.shape[1], dtype=jnp.int32) <= step_index
    cache_scores = jnp.where(cache_live[:, None, None, :], cache_scores, -1e+30)
    fresh_scores = jnp.where(fresh_live[None, None, None, :], fresh_scores, -1e+30)
    highest = jnp.maximum(lax.optimization_barrier(jnp.max(cache_scores, axis=-1)), lax.optimization_barrier(jnp.max(fresh_scores, axis=-1)))[..., None]
    cache_exp = jnp.exp(cache_scores - highest)
    fresh_exp = jnp.exp(fresh_scores - highest)
    denominator = lax.optimization_barrier(jnp.sum(cache_exp, axis=-1, keepdims=True)) + lax.optimization_barrier(jnp.sum(fresh_exp, axis=-1, keepdims=True))
    cache_probs = lax.optimization_barrier((cache_exp / denominator).astype(jnp.bfloat16)).astype(jnp.float32)
    fresh_probs = lax.optimization_barrier((fresh_exp / denominator).astype(jnp.bfloat16)).astype(jnp.float32)
    attended = jnp.einsum('rgqc,rcgd->rgqd', cache_probs, cache_values)
    attended = attended + jnp.einsum('rgqj,rjgd->rgqd', fresh_probs, fresh_values)
    return attended.reshape(row_count, HEADS * HEAD_DIM)

def one_expert(pieces):
    tokens_in, gate_w, up_w, down_w = pieces
    gate_part = jnp.dot(tokens_in.astype(jnp.float32), gate_w.astype(jnp.float32), preferred_element_type=jnp.float32)
    up_part = jnp.dot(tokens_in.astype(jnp.float32), up_w.astype(jnp.float32), preferred_element_type=jnp.float32)
    active = lax.optimization_barrier((jax.nn.silu(gate_part) * up_part).astype(jnp.bfloat16))
    result = jnp.dot(active.astype(jnp.float32), down_w.astype(jnp.float32).T, preferred_element_type=jnp.float32)
    return result.astype(jnp.bfloat16)

def expert_mix(normed, step_ids, weights, gate_half, up_half, down_half):
    device_count = N_NODE * N_LOCAL
    placer = jax.vmap(partial(place_rows, expert_count=EXPERTS, capacity=CAP))
    slot_map = placer(step_ids.reshape(device_count, R_DEV, TOPK))
    device_index = jnp.arange(device_count, dtype=jnp.int32)[:, None, None]
    row_index = jnp.arange(ROWS, dtype=jnp.int32).reshape(device_count, R_DEV, 1)
    source_rows = jnp.full((device_count, EXPERTS * CAP), ROWS, dtype=jnp.int32)
    source_rows = source_rows.at[device_index, slot_map].set(jnp.broadcast_to(row_index, slot_map.shape))
    padded = jnp.concatenate([normed, jnp.zeros((1, D), normed.dtype)], axis=0)
    packed = padded[source_rows]
    packed = packed.reshape(device_count, EXPERTS, CAP, D).transpose(1, 0, 2, 3).reshape(EXPERTS, device_count * CAP, D)
    served = lax.map(one_expert, (packed, gate_half, up_half, down_half))
    served = lax.optimization_barrier(served)
    returned = served.reshape(EXPERTS, device_count, CAP, D).transpose(1, 0, 2, 3).reshape(device_count, EXPERTS * CAP, D)
    picked = returned[device_index, slot_map].reshape(ROWS, TOPK, D)
    return lax.optimization_barrier(jnp.sum(weights[:, :, None] * picked.astype(jnp.float32), axis=1))

def reference(residual, query, new_keys, new_values, key_cache, value_cache, lengths, norm_gain, expert_ids, gate_scores, learner_gate, learner_up, learner_down):
    gate_half = learner_gate.astype(jnp.bfloat16)
    up_half = learner_up.astype(jnp.bfloat16)
    down_half = learner_down.astype(jnp.bfloat16)
    cache_keys = key_cache.astype(jnp.float32).reshape(ROWS, CACHE, KV_HEADS, HEAD_DIM)
    cache_values = value_cache.astype(jnp.float32).reshape(ROWS, CACHE, KV_HEADS, HEAD_DIM)
    fresh_keys = jnp.transpose(new_keys, (1, 0, 2)).astype(jnp.float32).reshape(ROWS, STEPS, KV_HEADS, HEAD_DIM)
    fresh_values = jnp.transpose(new_values, (1, 0, 2)).astype(jnp.float32).reshape(ROWS, STEPS, KV_HEADS, HEAD_DIM)
    mixtures = []
    streams = []
    for step_index in range(STEPS):
        attended = attend(query[step_index], cache_keys, cache_values, fresh_keys, fresh_values, lengths, step_index)
        hidden_state = residual[step_index].astype(jnp.float32) + attended
        mean_square = lax.optimization_barrier(jnp.mean(hidden_state * hidden_state, axis=-1, keepdims=True))
        normed = (hidden_state * lax.rsqrt(mean_square + epsilon) * norm_gain).astype(jnp.bfloat16)
        weights = gate_scores[step_index] / lax.optimization_barrier(jnp.sum(gate_scores[step_index], axis=-1, keepdims=True))
        mixture_sum = expert_mix(normed, expert_ids[step_index], weights, gate_half, up_half, down_half)
        mixtures.append(mixture_sum.astype(jnp.bfloat16))
        streams.append((hidden_state + mixture_sum).astype(jnp.bfloat16))
    return (jnp.stack(mixtures), jnp.stack(streams))
```

```python
import math

import jax
import jax.numpy as jnp
from jax import lax
from jax.sharding import PartitionSpec as P

HEADS = 16
KV_HEADS = 2
HEAD_DIM = 128


epsilon = 1e-06


def attend_all(query, key_cache, value_cache, new_keys, new_values, lengths):
    steps, row_count, _ = query.shape
    group_size = HEADS // KV_HEADS
    queries = query.reshape(steps, row_count, KV_HEADS, group_size, HEAD_DIM)
    queries = jnp.transpose(queries, (1, 2, 0, 3, 4)).reshape(
        row_count, KV_HEADS, steps * group_size, HEAD_DIM
    )
    keys = jnp.concatenate([key_cache, jnp.transpose(new_keys, (1, 0, 2))], axis=1)
    values = jnp.concatenate([value_cache, jnp.transpose(new_values, (1, 0, 2))], axis=1)
    slots = key_cache.shape[1]
    total = keys.shape[1]
    keys = keys.reshape(row_count, total, KV_HEADS, HEAD_DIM)
    values = values.reshape(row_count, total, KV_HEADS, HEAD_DIM)
    scores = jnp.einsum(
        "rgqd,rcgd->rgqc", queries, keys, preferred_element_type=jnp.float32
    ) * (1.0 / math.sqrt(HEAD_DIM))
    slot = jnp.arange(total, dtype=jnp.int32)[None, None, :]
    step = (jnp.arange(steps * group_size, dtype=jnp.int32) // group_size)[None, :, None]
    live = jnp.where(slot < slots, slot < lengths[:, None, None], slot - slots <= step)
    scores = jnp.where(live[:, None], scores, -1e30)
    highest = jnp.max(scores, axis=-1, keepdims=True)
    grown = jnp.exp(scores - highest)
    probs = (grown / jnp.sum(grown, axis=-1, keepdims=True)).astype(jnp.bfloat16)
    attended = jnp.einsum("rgqc,rcgd->rgqd", probs, values, preferred_element_type=jnp.float32)
    attended = attended.reshape(row_count, KV_HEADS, steps, group_size * HEAD_DIM)
    return jnp.transpose(attended, (2, 0, 1, 3)).reshape(steps, row_count, HEADS * HEAD_DIM)


def body(
    residual,
    query,
    new_keys,
    new_values,
    key_cache,
    value_cache,
    lengths,
    norm_gain,
    expert_ids,
    gate_scores,
    learner_gate,
    learner_up,
    learner_down,
):
    axes = ("node", "local")
    steps, row_count, width = residual.shape
    expert_total = learner_gate.shape[0]
    gate_w, up_w, down_w = (
        lax.all_to_all(w.astype(jnp.bfloat16), axes, split_axis=0, concat_axis=1, tiled=True)
        for w in (learner_gate, learner_up, learner_down)
    )
    attended = attend_all(query, key_cache, value_cache, new_keys, new_values, lengths)
    hidden = residual.astype(jnp.float32) + attended
    mean_square = jnp.mean(hidden * hidden, axis=-1, keepdims=True)
    normed = (hidden * lax.rsqrt(mean_square + epsilon) * norm_gain).astype(jnp.bfloat16)
    weights = gate_scores / jnp.sum(gate_scores, axis=-1, keepdims=True)
    chosen = expert_ids[..., None] == jnp.arange(expert_total, dtype=jnp.int32)
    dense = jnp.sum(jnp.where(chosen, weights[..., None], 0.0), axis=2)
    dense = dense.reshape(steps * row_count, expert_total)
    rows = lax.all_gather(normed.reshape(steps * row_count, width), axes, axis=0, tiled=True)
    owned = gate_w.shape[0]
    shares = lax.all_to_all(dense, axes, split_axis=1, concat_axis=0, tiled=True)
    total = None
    for j in range(owned):
        gate_part = jnp.dot(rows, gate_w[j], preferred_element_type=jnp.float32)
        up_part = jnp.dot(rows, up_w[j], preferred_element_type=jnp.float32)
        active = (jax.nn.silu(gate_part) * up_part).astype(jnp.bfloat16)
        served = lax.dot_general(
            active, down_w[j], (((1,), (1,)), ((), ())), preferred_element_type=jnp.float32
        )
        served = served * shares[:, j : j + 1]
        total = served if total is None else total + served
    summed = lax.psum_scatter(total.astype(jnp.bfloat16), axes, scatter_dimension=0, tiled=True)
    mixture_sum = summed.astype(jnp.float32).reshape(residual.shape)
    return (mixture_sum.astype(jnp.bfloat16), (hidden + mixture_sum).astype(jnp.bfloat16))


def solution(mesh):
    return jax.shard_map(
        body,
        mesh=mesh,
        in_specs=(
            P(None, ("groups", "node", "local"), None),
            P(None, ("groups", "node", "local"), None),
            P(None, ("groups", "node", "local"), None),
            P(None, ("groups", "node", "local"), None),
            P(("groups", "node", "local"), None, None),
            P(("groups", "node", "local"), None, None),
            P(("groups", "node", "local")),
            P(),
            P(None, ("groups", "node", "local"), None),
            P(None, ("groups", "node", "local"), None),
            P(None, ("node", "local"), None),
            P(None, ("node", "local"), None),
            P(None, ("node", "local"), None),
        ),
        out_specs=(
            P(None, ("groups", "node", "local"), None),
            P(None, ("groups", "node", "local"), None),
        ),
        check_vma=False,
    )
```

```python
import functools
import math

import jax
import jax.numpy as jnp
from jax import lax
from jax.experimental import pallas as pl
from jax.experimental.pallas import tpu as pltpu
from jax.sharding import PartitionSpec as P

HEADS = 16
KV_HEADS = 2
HEAD_DIM = 128


epsilon = 1e-06


def attend_all(query, key_cache, value_cache, new_keys, new_values, lengths):
    steps, row_count, _ = query.shape
    group_size = HEADS // KV_HEADS
    queries = query.reshape(steps, row_count, KV_HEADS, group_size, HEAD_DIM)
    queries = jnp.transpose(queries, (1, 2, 0, 3, 4)).reshape(
        row_count, KV_HEADS, steps * group_size, HEAD_DIM
    )
    keys = jnp.concatenate([key_cache, jnp.transpose(new_keys, (1, 0, 2))], axis=1)
    values = jnp.concatenate([value_cache, jnp.transpose(new_values, (1, 0, 2))], axis=1)
    slots = key_cache.shape[1]
    total = keys.shape[1]
    keys = keys.reshape(row_count, total, KV_HEADS, HEAD_DIM)
    values = values.reshape(row_count, total, KV_HEADS, HEAD_DIM)
    scores = jnp.einsum(
        "rgqd,rcgd->rgqc", queries, keys, preferred_element_type=jnp.float32
    ) * (1.0 / math.sqrt(HEAD_DIM))
    slot = jnp.arange(total, dtype=jnp.int32)[None, None, :]
    step = (jnp.arange(steps * group_size, dtype=jnp.int32) // group_size)[None, :, None]
    live = jnp.where(slot < slots, slot < lengths[:, None, None], slot - slots <= step)
    scores = jnp.where(live[:, None], scores, -1e30)
    highest = jnp.max(scores, axis=-1, keepdims=True)
    grown = jnp.exp(scores - highest)
    probs = (grown / jnp.sum(grown, axis=-1, keepdims=True)).astype(jnp.bfloat16)
    attended = jnp.einsum("rgqc,rcgd->rgqd", probs, values, preferred_element_type=jnp.float32)
    attended = attended.reshape(row_count, KV_HEADS, steps, group_size * HEAD_DIM)
    return jnp.transpose(attended, (2, 0, 1, 3)).reshape(steps, row_count, HEADS * HEAD_DIM)


MESH = pl.DeviceIdType.MESH


def flip_low(v):
    return v + 1 - 2 * lax.rem(v, 2)


def flip_high(v):
    return v + 2 - 4 * (v // 2)


def flip(v, bits):
    v = flip_low(v) if bits % 2 else v
    return flip_high(v) if bits >= 2 else v


CROSS = [(dn, dl) for dl in (2, 3) for dn in (0, 1, 2, 3)]
SAME = [(dn, dl) for dl in (0, 1) for dn in (0, 1, 2, 3)]


def moe_kernel(
    normed, share, lg, lu, ld, out,
    stage_x, stage_s, send_x, send_s, wbuf, rows, part, rbuf, shares,
    load_x, load_s, xs, xr, ss, sr, fs, fr, hs, hr, ags, agr, rss, rsr,
):
    g, n, l = lax.axis_index("groups"), lax.axis_index("node"), lax.axis_index("local")
    me = n * 4 + l
    core, x = lax.rem(n, 2), n // 2
    block = core * 8 + x * 4 + lax.rem(l, 2) * 2 + l // 2
    steps, held, width = normed.shape
    depth = lg.shape[1]
    half = depth // 2
    mine = pl.ds(pl.multiple_of(g * half, half), half)

    def peer(dn, dl):
        return flip(n, dn), flip(l, dl)

    def to(dn, dl):
        pn, plo = peer(dn, dl)
        return (g, pn, plo)

    learners = (lg, lu, ld)

    def loads(i, cross):
        dn, dl = (CROSS if cross else SAME)[i]
        pn, plo = peer(dn, dl)
        p = pn * 4 + plo
        made = []
        for a, ref in enumerate(learners):
            if cross:
                made.append(pltpu.make_async_copy(ref.at[p, mine], stage_x.at[i, a], load_x.at[i, a]))
            else:
                made.append(pltpu.make_async_copy(ref.at[p], stage_s.at[i, a], load_s.at[i, a]))
        return made

    for i in range(8):
        for c in loads(i, True):
            c.start()
    for i in range(8):
        for c in loads(i, False):
            c.start()

    barrier = pltpu.get_barrier_semaphore()
    everyone = [to(dn, dl) for dn, dl in CROSS + SAME[1:]] + [(1 - g, n, l)]
    for who in everyone:
        pl.semaphore_signal(barrier, inc=1, device_id=who, device_id_type=MESH)
    for t in range(steps):
        rows[t, block] = normed[t]
    shares[me] = share[me]
    pl.semaphore_wait(barrier, len(everyone))

    HOPS = ((0, 2), (0, 1), (2, 0), (1, 0))

    def gather(k, t):
        size = 1 << k
        base = block // size * size
        ref = rows.at[t, pl.ds(base, size)]
        return pltpu.make_async_remote_copy(
            src_ref=ref, dst_ref=ref, send_sem=ags.at[k, t], recv_sem=agr.at[k, t],
            device_id=to(*HOPS[k]), device_id_type=MESH,
        )

    OFFSET = (14, 12, 8, 0)

    def scatter(k, t):
        size = 1 << k
        mybase = block // size * size
        base = mybase + size - 2 * size * lax.rem(block // size, 2)
        return pltpu.make_async_remote_copy(
            src_ref=part.at[t, pl.ds(base, size)], dst_ref=rbuf.at[t, pl.ds(OFFSET[k], size)],
            send_sem=rss.at[k, t], recv_sem=rsr.at[k, t],
            device_id=to(*HOPS[k]), device_id_type=MESH,
        )

    def share_copy(i):
        dn, dl = (CROSS + SAME)[i]
        pn, plo = peer(dn, dl)
        return pltpu.make_async_remote_copy(
            src_ref=share.at[pn * 4 + plo], dst_ref=shares.at[me], send_sem=hs.at[i], recv_sem=hr.at[i],
            device_id=(g, pn, plo), device_id_type=MESH,
        )

    def cross_copy(i):
        return pltpu.make_async_remote_copy(
            src_ref=send_x.at[i], dst_ref=wbuf.at[:, me, mine], send_sem=xs.at[i], recv_sem=xr.at[i],
            device_id=to(*CROSS[i]), device_id_type=MESH,
        )

    def same_copy(i):
        return pltpu.make_async_remote_copy(
            src_ref=send_s.at[i], dst_ref=wbuf.at[:, me], send_sem=ss.at[i], recv_sem=sr.at[i],
            device_id=to(*SAME[i]), device_id_type=MESH,
        )

    def forward(i):
        pn, plo = peer(*CROSS[i])
        ref = wbuf.at[:, pn * 4 + plo, mine]
        return pltpu.make_async_remote_copy(
            src_ref=ref, dst_ref=ref, send_sem=fs.at[i], recv_sem=fr.at[i],
            device_id=(1 - g, n, l), device_id_type=MESH,
        )

    for t in range(steps):
        gather(0, t).start()
    for i in range(16):
        if i != 8:
            share_copy(i).start()
    for i in range(8):
        for c in loads(i, True):
            c.wait()
        send_x[i] = stage_x[i].astype(jnp.bfloat16)
        cross_copy(i).start()
    for i in range(1, 8):
        for c in loads(i, False):
            c.wait()
        send_s[i] = stage_s[i].astype(jnp.bfloat16)
        same_copy(i).start()
    for c in loads(0, False):
        c.wait()
    wbuf[:, me] = stage_s[0].astype(jnp.bfloat16)

    for t in range(steps):
        gather(0, t).wait_recv()
        gather(1, t).start()
    for i in range(4):
        cross_copy(i).wait_recv()
        forward(i).start()
    for t in range(steps):
        gather(1, t).wait_recv()
        gather(2, t).start()
    for i in range(4, 8):
        cross_copy(i).wait_recv()
        forward(i).start()
    for t in range(steps):
        gather(2, t).wait_recv()
        gather(3, t).start()
    for i in range(16):
        if i != 8:
            share_copy(i).wait_recv()
    for i in range(1, 8):
        same_copy(i).wait_recv()
    for i in range(8):
        forward(i).wait_recv()
    for t in range(steps):
        gather(3, t).wait_recv()

    count = 16 * held
    hidden_units = lg.shape[2]
    eye = lax.broadcasted_iota(jnp.int32, (held, 128), 0)
    lane = lax.broadcasted_iota(jnp.int32, (held, 128), 1)

    def compute(t):
        tokens = rows[t].reshape(count, width)
        gate_part = jnp.dot(tokens, wbuf[0].reshape(width, hidden_units), preferred_element_type=jnp.float32)
        up_part = jnp.dot(tokens, wbuf[1].reshape(width, hidden_units), preferred_element_type=jnp.float32)
        active = (gate_part / (1.0 + jnp.exp(-gate_part)) * up_part).astype(jnp.bfloat16)
        columns = []
        for b in range(16):
            bc, bx, bl = b // 8, b // 4 % 2, (b // 2 % 2) + 2 * (b % 2)
            source = (bx * 2 + bc) * 4 + bl
            line = shares[source, 0:1, :]
            picked = jnp.where(lane == eye + t * held, line, 0.0)
            columns.append(jnp.sum(picked, axis=1, keepdims=True))
        column = jnp.concatenate(columns, axis=0)
        for j in range(4):
            wide = width // 4
            down = wbuf[2, 4 * j : 4 * j + 4].reshape(wide, hidden_units)
            served = lax.dot_general(
                active, down, (((1,), (1,)), ((), ())), preferred_element_type=jnp.float32
            )
            part[t, :, :, wide * j : wide * (j + 1)] = (
                (served * column).astype(jnp.bfloat16).reshape(16, held, wide)
            )

    def reduce(k, t):
        size = 1 << k
        base = block // size * size
        scatter(k, t).wait_recv()
        total = part[t, pl.ds(base, size)].astype(jnp.float32) + rbuf[
            t, OFFSET[k] : OFFSET[k] + size
        ].astype(jnp.float32)
        if k == 0:
            out[t] = total[0]
        else:
            part[t, pl.ds(base, size)] = total.astype(jnp.bfloat16)
            scatter(k - 1, t).start()

    def turn(t, carry):
        compute(t)
        scatter(3, t).start()

        @pl.when(t >= 1)
        def _():
            reduce(3, t - 1)

        return carry

    lax.fori_loop(0, steps, turn, 0)
    reduce(3, steps - 1)
    for k in (2, 1, 0):
        for t in range(steps):
            reduce(k, t)

    for t in range(steps):
        for k in range(4):
            gather(k, t).wait_send()
            scatter(k, t).wait_send()
    for i in range(16):
        if i != 8:
            share_copy(i).wait_send()
    for i in range(8):
        cross_copy(i).wait_send()
        forward(i).wait_send()
    for i in range(1, 8):
        same_copy(i).wait_send()


def kernel_call(normed, share, lg, lu, ld):
    steps, held, width = normed.shape
    experts, depth, units = lg.shape
    bf16, f32 = jnp.bfloat16, jnp.float32
    vmem = pl.BlockSpec(memory_space=pltpu.VMEM)
    hbm = pl.BlockSpec(memory_space=pl.ANY)
    dma = pltpu.SemaphoreType.DMA
    return pl.pallas_call(
        moe_kernel,
        out_shape=jax.ShapeDtypeStruct((steps, held, width), f32),
        in_specs=[vmem, vmem, hbm, hbm, hbm],
        out_specs=vmem,
        scratch_shapes=[
            pltpu.VMEM((8, 3, depth // 2, units), f32),
            pltpu.VMEM((8, 3, depth, units), f32),
            pltpu.VMEM((8, 3, depth // 2, units), bf16),
            pltpu.VMEM((8, 3, depth, units), bf16),
            pltpu.VMEM((3, 16, depth, units), bf16),
            pltpu.VMEM((steps, 16, held, width), bf16),
            pltpu.VMEM((steps, 16, held, width), bf16),
            pltpu.VMEM((steps, 15, held, width), bf16),
            pltpu.VMEM((16, 8, 128), f32),
            dma((8, 3)), dma((8, 3)),
            dma((8,)), dma((8,)), dma((8,)), dma((8,)), dma((8,)), dma((8,)),
            dma((16,)), dma((16,)),
            dma((4, steps)), dma((4, steps)), dma((4, steps)), dma((4, steps)),
        ],
        compiler_params=pltpu.CompilerParams(
            collective_id=0, has_side_effects=True, vmem_limit_bytes=56 * 1024 * 1024
        ),
    )(normed, share, lg, lu, ld)


def plain_mix(normed, dense, learner_gate, learner_up, learner_down):
    axes = ("node", "local")
    steps, row_count, width = normed.shape
    gate_w, up_w, down_w = (
        lax.all_to_all(w.astype(jnp.bfloat16), axes, split_axis=0, concat_axis=1, tiled=True)
        for w in (learner_gate, learner_up, learner_down)
    )
    rows = lax.all_gather(normed.reshape(steps * row_count, width), axes, axis=0, tiled=True)
    owned = gate_w.shape[0]
    shares = lax.all_to_all(dense, axes, split_axis=1, concat_axis=0, tiled=True)
    total = None
    for j in range(owned):
        gate_part = jnp.dot(rows, gate_w[j], preferred_element_type=jnp.float32)
        up_part = jnp.dot(rows, up_w[j], preferred_element_type=jnp.float32)
        active = (jax.nn.silu(gate_part) * up_part).astype(jnp.bfloat16)
        served = lax.dot_general(
            active, down_w[j], (((1,), (1,)), ((), ())), preferred_element_type=jnp.float32
        )
        served = served * shares[:, j : j + 1]
        total = served if total is None else total + served
    summed = lax.psum_scatter(total.astype(jnp.bfloat16), axes, scatter_dimension=0, tiled=True)
    return summed.astype(jnp.float32).reshape(normed.shape)


def body(
    fused,
    residual,
    query,
    new_keys,
    new_values,
    key_cache,
    value_cache,
    lengths,
    norm_gain,
    expert_ids,
    gate_scores,
    learner_gate,
    learner_up,
    learner_down,
):
    steps, row_count, width = residual.shape
    expert_total = learner_gate.shape[0]
    attended = attend_all(query, key_cache, value_cache, new_keys, new_values, lengths)
    hidden = residual.astype(jnp.float32) + attended
    mean_square = jnp.mean(hidden * hidden, axis=-1, keepdims=True)
    normed = (hidden * lax.rsqrt(mean_square + epsilon) * norm_gain).astype(jnp.bfloat16)
    weights = gate_scores / jnp.sum(gate_scores, axis=-1, keepdims=True)
    chosen = expert_ids[..., None] == jnp.arange(expert_total, dtype=jnp.int32)
    dense = jnp.sum(jnp.where(chosen, weights[..., None], 0.0), axis=2)
    dense = dense.reshape(steps * row_count, expert_total)
    if fused:
        share = jnp.pad(dense.T, ((0, 0), (0, 128 - steps * row_count)))
        share = jnp.broadcast_to(share[:, None, :], (expert_total, 8, 128))
        mixture_sum = kernel_call(normed, share, learner_gate, learner_up, learner_down)
    else:
        mixture_sum = plain_mix(normed, dense, learner_gate, learner_up, learner_down)
    return (mixture_sum.astype(jnp.bfloat16), (hidden + mixture_sum).astype(jnp.bfloat16))


def solution(mesh):
    sizes = dict(mesh.shape)
    fused = sizes == {"groups": 2, "node": 4, "local": 4}
    return jax.shard_map(
        functools.partial(body, fused),
        mesh=mesh,
        in_specs=(
            P(None, ("groups", "node", "local"), None),
            P(None, ("groups", "node", "local"), None),
            P(None, ("groups", "node", "local"), None),
            P(None, ("groups", "node", "local"), None),
            P(("groups", "node", "local"), None, None),
            P(("groups", "node", "local"), None, None),
            P(("groups", "node", "local")),
            P(),
            P(None, ("groups", "node", "local"), None),
            P(None, ("groups", "node", "local"), None),
            P(None, ("node", "local"), None),
            P(None, ("node", "local"), None),
            P(None, ("node", "local"), None),
        ),
        out_specs=(
            P(None, ("groups", "node", "local"), None),
            P(None, ("groups", "node", "local"), None),
        ),
        check_vma=False,
    )
```

```python
import functools
import math

import jax
import jax.numpy as jnp
from jax import lax
from jax.experimental import pallas as pl
from jax.experimental.pallas import tpu as pltpu
from jax.sharding import PartitionSpec as P

HEADS = 16
KV_HEADS = 2
HEAD_DIM = 128


epsilon = 1e-06


def attend_all(query, key_cache, value_cache, new_keys, new_values, lengths):
    steps, row_count, _ = query.shape
    group_size = HEADS // KV_HEADS
    queries = query.reshape(steps, row_count, KV_HEADS, group_size, HEAD_DIM)
    queries = jnp.transpose(queries, (1, 2, 0, 3, 4)).reshape(
        row_count, KV_HEADS, steps * group_size, HEAD_DIM
    )
    keys = jnp.concatenate([key_cache, jnp.transpose(new_keys, (1, 0, 2))], axis=1)
    values = jnp.concatenate([value_cache, jnp.transpose(new_values, (1, 0, 2))], axis=1)
    slots = key_cache.shape[1]
    total = keys.shape[1]
    keys = keys.reshape(row_count, total, KV_HEADS, HEAD_DIM)
    values = values.reshape(row_count, total, KV_HEADS, HEAD_DIM)
    scores = jnp.einsum(
        "rgqd,rcgd->rgqc", queries, keys, preferred_element_type=jnp.float32
    ) * (1.0 / math.sqrt(HEAD_DIM))
    slot = jnp.arange(total, dtype=jnp.int32)[None, None, :]
    step = (jnp.arange(steps * group_size, dtype=jnp.int32) // group_size)[None, :, None]
    live = jnp.where(slot < slots, slot < lengths[:, None, None], slot - slots <= step)
    scores = jnp.where(live[:, None], scores, -1e30)
    highest = jnp.max(scores, axis=-1, keepdims=True)
    grown = jnp.exp(scores - highest)
    probs = (grown / jnp.sum(grown, axis=-1, keepdims=True)).astype(jnp.bfloat16)
    attended = jnp.einsum("rgqc,rcgd->rgqd", probs, values, preferred_element_type=jnp.float32)
    attended = attended.reshape(row_count, KV_HEADS, steps, group_size * HEAD_DIM)
    return jnp.transpose(attended, (2, 0, 1, 3)).reshape(steps, row_count, HEADS * HEAD_DIM)


MESH = pl.DeviceIdType.MESH


def flip_low(v):
    return v + 1 - 2 * lax.rem(v, 2)


def flip_high(v):
    return v + 2 - 4 * (v // 2)


def flip(v, bits):
    v = flip_low(v) if bits % 2 else v
    return flip_high(v) if bits >= 2 else v


CROSS = [(dn, dl) for dl in (2, 3, 1) for dn in (0, 1, 2, 3)]
SAME = [(dn, 0) for dn in (0, 1, 2, 3)]
FAR, NEAR = len(CROSS), len(SAME)


def moe_kernel(
    normed, share, lg, lu, ld, out,
    stage_x, stage_s, send_x, send_s, wbuf, rows, part, rbuf, shares,
    load_x, load_s, xs, xr, ss, sr, fs, fr, hs, hr, ags, agr, rss, rsr,
):
    g, n, l = lax.axis_index("groups"), lax.axis_index("node"), lax.axis_index("local")
    me = n * 4 + l
    core, x = lax.rem(n, 2), n // 2
    block = core * 8 + x * 4 + lax.rem(l, 2) * 2 + l // 2
    steps, held, width = normed.shape
    depth = lg.shape[1]
    half = depth // 2
    mine = pl.ds(pl.multiple_of(g * half, half), half)

    def peer(dn, dl):
        return flip(n, dn), flip(l, dl)

    def to(dn, dl):
        pn, plo = peer(dn, dl)
        return (g, pn, plo)

    learners = (lg, lu, ld)

    def loads(i, cross):
        dn, dl = (CROSS if cross else SAME)[i]
        pn, plo = peer(dn, dl)
        p = pn * 4 + plo
        made = []
        for a, ref in enumerate(learners):
            if cross:
                made.append(pltpu.make_async_copy(ref.at[p, mine], stage_x.at[i, a], load_x.at[i, a]))
            else:
                made.append(pltpu.make_async_copy(ref.at[p], stage_s.at[i, a], load_s.at[i, a]))
        return made

    for i in range(FAR):
        for c in loads(i, True):
            c.start()
    for i in range(NEAR):
        for c in loads(i, False):
            c.start()

    barrier = pltpu.get_barrier_semaphore()
    everyone = [to(dn, dl) for dn, dl in CROSS + SAME[1:]] + [(1 - g, n, l)]
    for who in everyone:
        pl.semaphore_signal(barrier, inc=1, device_id=who, device_id_type=MESH)
    for t in range(steps):
        rows[t, block] = normed[t]
    shares[me] = share[me]
    pl.semaphore_wait(barrier, len(everyone))

    HOPS = ((0, 2), (0, 1), (2, 0), (1, 0))

    def gather(k, t):
        size = 1 << k
        base = block // size * size
        ref = rows.at[t, pl.ds(base, size)]
        return pltpu.make_async_remote_copy(
            src_ref=ref, dst_ref=ref, send_sem=ags.at[k, t], recv_sem=agr.at[k, t],
            device_id=to(*HOPS[k]), device_id_type=MESH,
        )

    OFFSET = (14, 12, 8, 0)

    def scatter(k, t):
        size = 1 << k
        mybase = block // size * size
        base = mybase + size - 2 * size * lax.rem(block // size, 2)
        return pltpu.make_async_remote_copy(
            src_ref=part.at[t, pl.ds(base, size)], dst_ref=rbuf.at[t, pl.ds(OFFSET[k], size)],
            send_sem=rss.at[k, t], recv_sem=rsr.at[k, t],
            device_id=to(*HOPS[k]), device_id_type=MESH,
        )

    def share_copy(i):
        dn, dl = (CROSS + SAME)[i]
        pn, plo = peer(dn, dl)
        return pltpu.make_async_remote_copy(
            src_ref=share.at[pn * 4 + plo], dst_ref=shares.at[me], send_sem=hs.at[i], recv_sem=hr.at[i],
            device_id=(g, pn, plo), device_id_type=MESH,
        )

    def cross_copy(i):
        return pltpu.make_async_remote_copy(
            src_ref=send_x.at[i], dst_ref=wbuf.at[:, me, mine], send_sem=xs.at[i], recv_sem=xr.at[i],
            device_id=to(*CROSS[i]), device_id_type=MESH,
        )

    def same_copy(i):
        return pltpu.make_async_remote_copy(
            src_ref=send_s.at[i], dst_ref=wbuf.at[:, me], send_sem=ss.at[i], recv_sem=sr.at[i],
            device_id=to(*SAME[i]), device_id_type=MESH,
        )

    def forward(i):
        pn, plo = peer(*CROSS[i])
        ref = wbuf.at[:, pn * 4 + plo, mine]
        return pltpu.make_async_remote_copy(
            src_ref=ref, dst_ref=ref, send_sem=fs.at[i], recv_sem=fr.at[i],
            device_id=(1 - g, n, l), device_id_type=MESH,
        )

    for t in range(steps):
        gather(0, t).start()
    for i in range(16):
        if i != FAR:
            share_copy(i).start()
    def send_cross(lo, hi):
        for i in range(lo, hi):
            for c in loads(i, True):
                c.wait()
            send_x[i] = stage_x[i].astype(jnp.bfloat16)
            cross_copy(i).start()

    def pass_on(lo, hi):
        for i in range(lo, hi):
            cross_copy(i).wait_recv()
            forward(i).start()

    def next_hop(k):
        for t in range(steps):
            gather(k, t).wait_recv()
            gather(k + 1, t).start()

    send_cross(0, 4)
    next_hop(0)
    send_cross(4, 8)
    next_hop(1)
    send_cross(8, 12)
    pass_on(0, 4)
    next_hop(2)
    for i in range(1, NEAR):
        for c in loads(i, False):
            c.wait()
        send_s[i] = stage_s[i].astype(jnp.bfloat16)
        same_copy(i).start()
    for c in loads(0, False):
        c.wait()
    wbuf[:, me] = stage_s[0].astype(jnp.bfloat16)
    pass_on(4, FAR)
    for i in range(16):
        if i != FAR:
            share_copy(i).wait_recv()
    for i in range(1, NEAR):
        same_copy(i).wait_recv()
    for i in range(FAR):
        forward(i).wait_recv()
    for t in range(steps):
        gather(3, t).wait_recv()

    count = 16 * held
    hidden_units = lg.shape[2]
    eye = lax.broadcasted_iota(jnp.int32, (held, 128), 0)
    lane = lax.broadcasted_iota(jnp.int32, (held, 128), 1)

    def compute(t):
        tokens = rows[t].reshape(count, width)
        gate_part = jnp.dot(tokens, wbuf[0].reshape(width, hidden_units), preferred_element_type=jnp.float32)
        up_part = jnp.dot(tokens, wbuf[1].reshape(width, hidden_units), preferred_element_type=jnp.float32)
        active = (gate_part / (1.0 + jnp.exp(-gate_part)) * up_part).astype(jnp.bfloat16)
        columns = []
        for b in range(16):
            bc, bx, bl = b // 8, b // 4 % 2, (b // 2 % 2) + 2 * (b % 2)
            source = (bx * 2 + bc) * 4 + bl
            line = shares[source, 0:1, :]
            picked = jnp.where(lane == eye + t * held, line, 0.0)
            columns.append(jnp.sum(picked, axis=1, keepdims=True))
        column = jnp.concatenate(columns, axis=0)
        for j in range(4):
            wide = width // 4
            down = wbuf[2, 4 * j : 4 * j + 4].reshape(wide, hidden_units)
            served = lax.dot_general(
                active, down, (((1,), (1,)), ((), ())), preferred_element_type=jnp.float32
            )
            part[t, :, :, wide * j : wide * (j + 1)] = (
                (served * column).astype(jnp.bfloat16).reshape(16, held, wide)
            )

    def reduce(k, t):
        size = 1 << k
        base = block // size * size
        scatter(k, t).wait_recv()
        total = part[t, pl.ds(base, size)].astype(jnp.float32) + rbuf[
            t, OFFSET[k] : OFFSET[k] + size
        ].astype(jnp.float32)
        if k == 0:
            out[t] = total[0]
        else:
            part[t, pl.ds(base, size)] = total.astype(jnp.bfloat16)
            scatter(k - 1, t).start()

    def turn(t, carry):
        compute(t)
        scatter(3, t).start()

        @pl.when(t >= 1)
        def _():
            reduce(3, t - 1)

        return carry

    lax.fori_loop(0, steps, turn, 0)
    reduce(3, steps - 1)
    for k in (2, 1, 0):
        for t in range(steps):
            reduce(k, t)

    for t in range(steps):
        for k in range(4):
            gather(k, t).wait_send()
            scatter(k, t).wait_send()
    for i in range(16):
        if i != FAR:
            share_copy(i).wait_send()
    for i in range(FAR):
        cross_copy(i).wait_send()
        forward(i).wait_send()
    for i in range(1, NEAR):
        same_copy(i).wait_send()


def kernel_call(normed, share, lg, lu, ld):
    steps, held, width = normed.shape
    experts, depth, units = lg.shape
    bf16, f32 = jnp.bfloat16, jnp.float32
    vmem = pl.BlockSpec(memory_space=pltpu.VMEM)
    hbm = pl.BlockSpec(memory_space=pl.ANY)
    dma = pltpu.SemaphoreType.DMA
    return pl.pallas_call(
        moe_kernel,
        out_shape=jax.ShapeDtypeStruct((steps, held, width), f32),
        in_specs=[vmem, vmem, hbm, hbm, hbm],
        out_specs=vmem,
        scratch_shapes=[
            pltpu.VMEM((FAR, 3, depth // 2, units), f32),
            pltpu.VMEM((NEAR, 3, depth, units), f32),
            pltpu.VMEM((FAR, 3, depth // 2, units), bf16),
            pltpu.VMEM((NEAR, 3, depth, units), bf16),
            pltpu.VMEM((3, 16, depth, units), bf16),
            pltpu.VMEM((steps, 16, held, width), bf16),
            pltpu.VMEM((steps, 16, held, width), bf16),
            pltpu.VMEM((steps, 15, held, width), bf16),
            pltpu.VMEM((16, 8, 128), f32),
            dma((FAR, 3)), dma((NEAR, 3)),
            dma((FAR,)), dma((FAR,)), dma((NEAR,)), dma((NEAR,)), dma((FAR,)), dma((FAR,)),
            dma((16,)), dma((16,)),
            dma((4, steps)), dma((4, steps)), dma((4, steps)), dma((4, steps)),
        ],
        compiler_params=pltpu.CompilerParams(
            collective_id=0, has_side_effects=True, vmem_limit_bytes=56 * 1024 * 1024
        ),
    )(normed, share, lg, lu, ld)


def plain_mix(normed, dense, learner_gate, learner_up, learner_down):
    axes = ("node", "local")
    steps, row_count, width = normed.shape
    gate_w, up_w, down_w = (
        lax.all_to_all(w.astype(jnp.bfloat16), axes, split_axis=0, concat_axis=1, tiled=True)
        for w in (learner_gate, learner_up, learner_down)
    )
    rows = lax.all_gather(normed.reshape(steps * row_count, width), axes, axis=0, tiled=True)
    owned = gate_w.shape[0]
    shares = lax.all_to_all(dense, axes, split_axis=1, concat_axis=0, tiled=True)
    total = None
    for j in range(owned):
        gate_part = jnp.dot(rows, gate_w[j], preferred_element_type=jnp.float32)
        up_part = jnp.dot(rows, up_w[j], preferred_element_type=jnp.float32)
        active = (jax.nn.silu(gate_part) * up_part).astype(jnp.bfloat16)
        served = lax.dot_general(
            active, down_w[j], (((1,), (1,)), ((), ())), preferred_element_type=jnp.float32
        )
        served = served * shares[:, j : j + 1]
        total = served if total is None else total + served
    summed = lax.psum_scatter(total.astype(jnp.bfloat16), axes, scatter_dimension=0, tiled=True)
    return summed.astype(jnp.float32).reshape(normed.shape)


def body(
    fused,
    residual,
    query,
    new_keys,
    new_values,
    key_cache,
    value_cache,
    lengths,
    norm_gain,
    expert_ids,
    gate_scores,
    learner_gate,
    learner_up,
    learner_down,
):
    steps, row_count, width = residual.shape
    expert_total = learner_gate.shape[0]
    attended = attend_all(query, key_cache, value_cache, new_keys, new_values, lengths)
    hidden = residual.astype(jnp.float32) + attended
    mean_square = jnp.mean(hidden * hidden, axis=-1, keepdims=True)
    normed = (hidden * lax.rsqrt(mean_square + epsilon) * norm_gain).astype(jnp.bfloat16)
    weights = gate_scores / jnp.sum(gate_scores, axis=-1, keepdims=True)
    chosen = expert_ids[..., None] == jnp.arange(expert_total, dtype=jnp.int32)
    dense = jnp.sum(jnp.where(chosen, weights[..., None], 0.0), axis=2)
    dense = dense.reshape(steps * row_count, expert_total)
    if fused:
        share = jnp.pad(dense.T, ((0, 0), (0, 128 - steps * row_count)))
        share = jnp.broadcast_to(share[:, None, :], (expert_total, 8, 128))
        mixture_sum = kernel_call(normed, share, learner_gate, learner_up, learner_down)
    else:
        mixture_sum = plain_mix(normed, dense, learner_gate, learner_up, learner_down)
    return (mixture_sum.astype(jnp.bfloat16), (hidden + mixture_sum).astype(jnp.bfloat16))


def solution(mesh):
    sizes = dict(mesh.shape)
    fused = sizes == {"groups": 2, "node": 4, "local": 4}
    return jax.shard_map(
        functools.partial(body, fused),
        mesh=mesh,
        in_specs=(
            P(None, ("groups", "node", "local"), None),
            P(None, ("groups", "node", "local"), None),
            P(None, ("groups", "node", "local"), None),
            P(None, ("groups", "node", "local"), None),
            P(("groups", "node", "local"), None, None),
            P(("groups", "node", "local"), None, None),
            P(("groups", "node", "local")),
            P(),
            P(None, ("groups", "node", "local"), None),
            P(None, ("groups", "node", "local"), None),
            P(None, ("node", "local"), None),
            P(None, ("node", "local"), None),
            P(None, ("node", "local"), None),
        ),
        out_specs=(
            P(None, ("groups", "node", "local"), None),
            P(None, ("groups", "node", "local"), None),
        ),
        check_vma=False,
    )
```

```python
import functools
import math

import jax
import jax.numpy as jnp
from jax import lax
from jax.experimental import pallas as pl
from jax.experimental.pallas import tpu as pltpu
from jax.sharding import PartitionSpec as P

HEADS = 16
KV_HEADS = 2
HEAD_DIM = 128


epsilon = 1e-06


def attend_all(query, key_cache, value_cache, new_keys, new_values, lengths):
    steps, row_count, _ = query.shape
    group_size = HEADS // KV_HEADS
    queries = query.reshape(steps, row_count, KV_HEADS, group_size, HEAD_DIM)
    queries = jnp.transpose(queries, (1, 2, 0, 3, 4)).reshape(
        row_count, KV_HEADS, steps * group_size, HEAD_DIM
    )
    keys = jnp.concatenate([key_cache, jnp.transpose(new_keys, (1, 0, 2))], axis=1)
    values = jnp.concatenate([value_cache, jnp.transpose(new_values, (1, 0, 2))], axis=1)
    slots = key_cache.shape[1]
    total = keys.shape[1]
    keys = keys.reshape(row_count, total, KV_HEADS, HEAD_DIM)
    values = values.reshape(row_count, total, KV_HEADS, HEAD_DIM)
    scores = jnp.einsum(
        "rgqd,rcgd->rgqc", queries, keys, preferred_element_type=jnp.float32
    ) * (1.0 / math.sqrt(HEAD_DIM))
    slot = jnp.arange(total, dtype=jnp.int32)[None, None, :]
    step = (jnp.arange(steps * group_size, dtype=jnp.int32) // group_size)[None, :, None]
    live = jnp.where(slot < slots, slot < lengths[:, None, None], slot - slots <= step)
    scores = jnp.where(live[:, None], scores, -1e30)
    highest = jnp.max(scores, axis=-1, keepdims=True)
    grown = jnp.exp(scores - highest)
    probs = (grown / jnp.sum(grown, axis=-1, keepdims=True)).astype(jnp.bfloat16)
    attended = jnp.einsum("rgqc,rcgd->rgqd", probs, values, preferred_element_type=jnp.float32)
    attended = attended.reshape(row_count, KV_HEADS, steps, group_size * HEAD_DIM)
    return jnp.transpose(attended, (2, 0, 1, 3)).reshape(steps, row_count, HEADS * HEAD_DIM)


MESH = pl.DeviceIdType.MESH


def flip_low(v):
    return v + 1 - 2 * lax.rem(v, 2)


def flip_high(v):
    return v + 2 - 4 * (v // 2)


def flip(v, bits):
    v = flip_low(v) if bits % 2 else v
    return flip_high(v) if bits >= 2 else v


CROSS = [(dn, dl) for dl in (2, 3) for dn in (0, 1, 2, 3)]
SAME = [(dn, dl) for dl in (0, 1) for dn in (0, 1, 2, 3)]


def moe_kernel(
    normed, share, lg, lu, ld, out,
    stage_x, stage_s, send_x, send_s, wbuf, rows, part, rbuf, shares,
    load_x, load_s, xs, xr, ss, sr, fs, fr, hs, hr, ags, agr, rss, rsr,
):
    g, n, l = lax.axis_index("groups"), lax.axis_index("node"), lax.axis_index("local")
    me = n * 4 + l
    core, x = lax.rem(n, 2), n // 2
    block = core * 8 + x * 4 + lax.rem(l, 2) * 2 + l // 2
    steps, held, width = normed.shape
    depth = lg.shape[1]
    half = depth // 2
    mine = pl.ds(pl.multiple_of(g * half, half), half)

    def peer(dn, dl):
        return flip(n, dn), flip(l, dl)

    def to(dn, dl):
        pn, plo = peer(dn, dl)
        return (g, pn, plo)

    learners = (lg, lu, ld)

    def loads(i, cross):
        dn, dl = (CROSS if cross else SAME)[i]
        pn, plo = peer(dn, dl)
        p = pn * 4 + plo
        made = []
        for a, ref in enumerate(learners):
            if cross:
                made.append(pltpu.make_async_copy(ref.at[p, mine], stage_x.at[i, a], load_x.at[i, a]))
            else:
                made.append(pltpu.make_async_copy(ref.at[p], stage_s.at[i, a], load_s.at[i, a]))
        return made

    for i in range(8):
        for c in loads(i, True):
            c.start()
    for i in range(8):
        for c in loads(i, False):
            c.start()

    barrier = pltpu.get_barrier_semaphore()
    everyone = [to(dn, dl) for dn, dl in CROSS + SAME[1:]] + [(1 - g, n, l)]
    for who in everyone:
        pl.semaphore_signal(barrier, inc=1, device_id=who, device_id_type=MESH)
    for t in range(steps):
        rows[t, block] = normed[t]
    shares[me] = share[me]
    pl.semaphore_wait(barrier, len(everyone))

    HOPS = ((0, 2), (0, 1), (2, 0), (1, 0))

    def gather(k, t):
        size = 1 << k
        base = block // size * size
        ref = rows.at[t, pl.ds(base, size)]
        return pltpu.make_async_remote_copy(
            src_ref=ref, dst_ref=ref, send_sem=ags.at[k, t], recv_sem=agr.at[k, t],
            device_id=to(*HOPS[k]), device_id_type=MESH,
        )

    OFFSET = (14, 12, 8, 0)

    def scatter(k, t):
        size = 1 << k
        mybase = block // size * size
        base = mybase + size - 2 * size * lax.rem(block // size, 2)
        return pltpu.make_async_remote_copy(
            src_ref=part.at[t, pl.ds(base, size)], dst_ref=rbuf.at[t, pl.ds(OFFSET[k], size)],
            send_sem=rss.at[k, t], recv_sem=rsr.at[k, t],
            device_id=to(*HOPS[k]), device_id_type=MESH,
        )

    def share_copy(i):
        dn, dl = (CROSS + SAME)[i]
        pn, plo = peer(dn, dl)
        return pltpu.make_async_remote_copy(
            src_ref=share.at[pn * 4 + plo], dst_ref=shares.at[me], send_sem=hs.at[i], recv_sem=hr.at[i],
            device_id=(g, pn, plo), device_id_type=MESH,
        )

    def cross_copy(i):
        return pltpu.make_async_remote_copy(
            src_ref=send_x.at[i], dst_ref=wbuf.at[:, me, mine], send_sem=xs.at[i], recv_sem=xr.at[i],
            device_id=to(*CROSS[i]), device_id_type=MESH,
        )

    def same_copy(i):
        return pltpu.make_async_remote_copy(
            src_ref=send_s.at[i], dst_ref=wbuf.at[:, me], send_sem=ss.at[i], recv_sem=sr.at[i],
            device_id=to(*SAME[i]), device_id_type=MESH,
        )

    def forward(i):
        pn, plo = peer(*CROSS[i])
        ref = wbuf.at[:, pn * 4 + plo, mine]
        return pltpu.make_async_remote_copy(
            src_ref=ref, dst_ref=ref, send_sem=fs.at[i], recv_sem=fr.at[i],
            device_id=(1 - g, n, l), device_id_type=MESH,
        )

    for t in range(steps):
        gather(0, t).start()
    for i in range(16):
        if i != 8:
            share_copy(i).start()
    for i in range(8):
        for c in loads(i, True):
            c.wait()
        send_x[i] = stage_x[i].astype(jnp.bfloat16)
        cross_copy(i).start()
    for i in range(1, 8):
        for c in loads(i, False):
            c.wait()
        send_s[i] = stage_s[i].astype(jnp.bfloat16)
        same_copy(i).start()
    for c in loads(0, False):
        c.wait()
    wbuf[:, me] = stage_s[0].astype(jnp.bfloat16)

    for wave in range(steps + 2):
        for k in range(3):
            t = wave - k
            if 0 <= t < steps:
                gather(k, t).wait_recv()
                gather(k + 1, t).start()
        if wave >= 2:
            for i in (2 * wave - 4, 2 * wave - 3):
                cross_copy(i).wait_recv()
                forward(i).start()
    for i in range(16):
        if i != 8:
            share_copy(i).wait_recv()
    for i in range(1, 8):
        same_copy(i).wait_recv()
    for i in range(8):
        forward(i).wait_recv()
    for t in range(steps):
        gather(3, t).wait_recv()

    count = 16 * held
    hidden_units = lg.shape[2]
    eye = lax.broadcasted_iota(jnp.int32, (held, 128), 0)
    lane = lax.broadcasted_iota(jnp.int32, (held, 128), 1)

    def compute(t):
        tokens = rows[t].reshape(count, width)
        gate_part = jnp.dot(tokens, wbuf[0].reshape(width, hidden_units), preferred_element_type=jnp.float32)
        up_part = jnp.dot(tokens, wbuf[1].reshape(width, hidden_units), preferred_element_type=jnp.float32)
        active = (gate_part / (1.0 + jnp.exp(-gate_part)) * up_part).astype(jnp.bfloat16)
        columns = []
        for b in range(16):
            bc, bx, bl = b // 8, b // 4 % 2, (b // 2 % 2) + 2 * (b % 2)
            source = (bx * 2 + bc) * 4 + bl
            line = shares[source, 0:1, :]
            picked = jnp.where(lane == eye + t * held, line, 0.0)
            columns.append(jnp.sum(picked, axis=1, keepdims=True))
        column = jnp.concatenate(columns, axis=0)
        for j in range(4):
            wide = width // 4
            down = wbuf[2, 4 * j : 4 * j + 4].reshape(wide, hidden_units)
            served = lax.dot_general(
                active, down, (((1,), (1,)), ((), ())), preferred_element_type=jnp.float32
            )
            part[t, :, :, wide * j : wide * (j + 1)] = (
                (served * column).astype(jnp.bfloat16).reshape(16, held, wide)
            )

    def reduce(k, t):
        size = 1 << k
        base = block // size * size
        scatter(k, t).wait_recv()
        total = part[t, pl.ds(base, size)].astype(jnp.float32) + rbuf[
            t, OFFSET[k] : OFFSET[k] + size
        ].astype(jnp.float32)
        if k == 0:
            out[t] = total[0]
        else:
            part[t, pl.ds(base, size)] = total.astype(jnp.bfloat16)
            scatter(k - 1, t).start()

    def turn(t, carry):
        compute(t)
        scatter(3, t).start()

        @pl.when(t >= 1)
        def _():
            reduce(3, t - 1)

        return carry

    lax.fori_loop(0, steps, turn, 0)
    reduce(3, steps - 1)
    for wave in range(steps + 2):
        for k in (2, 1, 0):
            t = wave - 2 + k
            if 0 <= t < steps:
                reduce(k, t)

    for t in range(steps):
        for k in range(4):
            gather(k, t).wait_send()
            scatter(k, t).wait_send()
    for i in range(16):
        if i != 8:
            share_copy(i).wait_send()
    for i in range(8):
        cross_copy(i).wait_send()
        forward(i).wait_send()
    for i in range(1, 8):
        same_copy(i).wait_send()


def kernel_call(normed, share, lg, lu, ld):
    steps, held, width = normed.shape
    experts, depth, units = lg.shape
    bf16, f32 = jnp.bfloat16, jnp.float32
    vmem = pl.BlockSpec(memory_space=pltpu.VMEM)
    hbm = pl.BlockSpec(memory_space=pl.ANY)
    dma = pltpu.SemaphoreType.DMA
    return pl.pallas_call(
        moe_kernel,
        out_shape=jax.ShapeDtypeStruct((steps, held, width), f32),
        in_specs=[vmem, vmem, hbm, hbm, hbm],
        out_specs=vmem,
        scratch_shapes=[
            pltpu.VMEM((8, 3, depth // 2, units), f32),
            pltpu.VMEM((8, 3, depth, units), f32),
            pltpu.VMEM((8, 3, depth // 2, units), bf16),
            pltpu.VMEM((8, 3, depth, units), bf16),
            pltpu.VMEM((3, 16, depth, units), bf16),
            pltpu.VMEM((steps, 16, held, width), bf16),
            pltpu.VMEM((steps, 16, held, width), bf16),
            pltpu.VMEM((steps, 15, held, width), bf16),
            pltpu.VMEM((16, 8, 128), f32),
            dma((8, 3)), dma((8, 3)),
            dma((8,)), dma((8,)), dma((8,)), dma((8,)), dma((8,)), dma((8,)),
            dma((16,)), dma((16,)),
            dma((4, steps)), dma((4, steps)), dma((4, steps)), dma((4, steps)),
        ],
        compiler_params=pltpu.CompilerParams(
            collective_id=0, has_side_effects=True, vmem_limit_bytes=56 * 1024 * 1024
        ),
    )(normed, share, lg, lu, ld)


def plain_mix(normed, dense, learner_gate, learner_up, learner_down):
    axes = ("node", "local")
    steps, row_count, width = normed.shape
    gate_w, up_w, down_w = (
        lax.all_to_all(w.astype(jnp.bfloat16), axes, split_axis=0, concat_axis=1, tiled=True)
        for w in (learner_gate, learner_up, learner_down)
    )
    rows = lax.all_gather(normed.reshape(steps * row_count, width), axes, axis=0, tiled=True)
    owned = gate_w.shape[0]
    shares = lax.all_to_all(dense, axes, split_axis=1, concat_axis=0, tiled=True)
    total = None
    for j in range(owned):
        gate_part = jnp.dot(rows, gate_w[j], preferred_element_type=jnp.float32)
        up_part = jnp.dot(rows, up_w[j], preferred_element_type=jnp.float32)
        active = (jax.nn.silu(gate_part) * up_part).astype(jnp.bfloat16)
        served = lax.dot_general(
            active, down_w[j], (((1,), (1,)), ((), ())), preferred_element_type=jnp.float32
        )
        served = served * shares[:, j : j + 1]
        total = served if total is None else total + served
    summed = lax.psum_scatter(total.astype(jnp.bfloat16), axes, scatter_dimension=0, tiled=True)
    return summed.astype(jnp.float32).reshape(normed.shape)


def body(
    fused,
    residual,
    query,
    new_keys,
    new_values,
    key_cache,
    value_cache,
    lengths,
    norm_gain,
    expert_ids,
    gate_scores,
    learner_gate,
    learner_up,
    learner_down,
):
    steps, row_count, width = residual.shape
    expert_total = learner_gate.shape[0]
    attended = attend_all(query, key_cache, value_cache, new_keys, new_values, lengths)
    hidden = residual.astype(jnp.float32) + attended
    mean_square = jnp.mean(hidden * hidden, axis=-1, keepdims=True)
    normed = (hidden * lax.rsqrt(mean_square + epsilon) * norm_gain).astype(jnp.bfloat16)
    weights = gate_scores / jnp.sum(gate_scores, axis=-1, keepdims=True)
    chosen = expert_ids[..., None] == jnp.arange(expert_total, dtype=jnp.int32)
    dense = jnp.sum(jnp.where(chosen, weights[..., None], 0.0), axis=2)
    dense = dense.reshape(steps * row_count, expert_total)
    if fused:
        share = jnp.pad(dense.T, ((0, 0), (0, 128 - steps * row_count)))
        share = jnp.broadcast_to(share[:, None, :], (expert_total, 8, 128))
        mixture_sum = kernel_call(normed, share, learner_gate, learner_up, learner_down)
    else:
        mixture_sum = plain_mix(normed, dense, learner_gate, learner_up, learner_down)
    return (mixture_sum.astype(jnp.bfloat16), (hidden + mixture_sum).astype(jnp.bfloat16))


def solution(mesh):
    sizes = dict(mesh.shape)
    fused = sizes == {"groups": 2, "node": 4, "local": 4}
    return jax.shard_map(
        functools.partial(body, fused),
        mesh=mesh,
        in_specs=(
            P(None, ("groups", "node", "local"), None),
            P(None, ("groups", "node", "local"), None),
            P(None, ("groups", "node", "local"), None),
            P(None, ("groups", "node", "local"), None),
            P(("groups", "node", "local"), None, None),
            P(("groups", "node", "local"), None, None),
            P(("groups", "node", "local")),
            P(),
            P(None, ("groups", "node", "local"), None),
            P(None, ("groups", "node", "local"), None),
            P(None, ("node", "local"), None),
            P(None, ("node", "local"), None),
            P(None, ("node", "local"), None),
        ),
        out_specs=(
            P(None, ("groups", "node", "local"), None),
            P(None, ("groups", "node", "local"), None),
        ),
        check_vma=False,
    )
```
